32 devices in a mesh: groups: 2 (over x), seq: 16 (over z, y, core).
Axes of the slice: x: 2, y: 2, z: 4, core: 2. Of those that a mesh axis runs over, the one named last changes fastest.
Arguments:
- out_grad: bfloat16 [2048, 4096], P(None, ('groups', 'seq')), parts along dimension 1, may hold values from -6 to 6
- gate_one: bfloat16 [2048, 4096], P(None, ('groups', 'seq')), parts along dimension 1, may hold values from -6 to 6
- gate_two: bfloat16 [2048, 4096], P(None, ('groups', 'seq')), parts along dimension 1, may hold values from -6 to 6
- conv_one: bfloat16 [2048, 4096], P(None, ('groups', 'seq')), parts along dimension 1, may hold values from -6 to 6
- conv_two: bfloat16 [2048, 4096], P(None, ('groups', 'seq')), parts along dimension 1, may hold values from -6 to 6
- value: bfloat16 [2048, 4096], P(None, ('groups', 'seq')), parts along dimension 1, may hold values from -6 to 6
- filter_one: float32 [2048, 2048], P('seq'), may hold values from -6 to 6
- filter_two: float32 [2048, 2048], P('seq'), may hold values from -6 to 6
- skip_one: float32 [2048], P('seq'), may hold values from -4 to 4
- skip_two: float32 [2048], P('seq'), may hold values from -4 to 4
- short_weight: float32 [2048, 3], replicated, may hold values from -3.5 to 3.5
Outputs:
- proj_grad: bfloat16 [2048, 4096], P(None, ('groups', 'seq')), parts along dimension 1
- gate_one_grad: bfloat16 [2048, 4096], P(None, ('groups', 'seq')), parts along dimension 1
- gate_two_grad: bfloat16 [2048, 4096], P(None, ('groups', 'seq')), parts along dimension 1
- filter_one_grad: float32 [4096, 2048], P(('groups', 'seq')), parts along dimension 0
- filter_two_grad: float32 [4096, 2048], P(('groups', 'seq')), parts along dimension 0
The draws below stay inside these ranges and needn't reach their ends.
There are 2 independent parts, one for each index of `groups`. The reference program is written for one: setup_inputs(seed, part) draws one part's arguments, and reference() takes and returns one part's arrays. A program takes and returns all parts, laid end to end along the dimension named above; an argument that names none is the same for every part. Nothing has to cross between parts.
All inputs are finite; a program needn't handle non-finite values.
Results may differ from the reference program's by a relative error of at most 0.0025.
Values may be sent and summed in bfloat16 or wider, within the bound.
No kernel may reach another device: no remote copies, remote signals or barrier semaphores. Data moves between devices by JAX's collectives and lax.ppermute only.
A program may use at most 128 MiB of HBM per device.

```python
import math
import jax
import jax.numpy as jnp
from jax import lax

D = 2048
KSHORT = 3
LENGTH = 2048


def level_of(own_key, extent, cuts, least, top_value):
    def one(dim, parts):
        steps = jax.random.uniform(jax.random.fold_in(jax.random.fold_in(own_key, 6), dim), (parts,), jnp.float32, least / len(cuts), top_value / len(cuts))
        return jnp.repeat(jnp.exp(steps), extent[dim] // parts).reshape((-1,) + (1,) * (len(extent) - dim - 1))

    factor_of = one(*cuts[0])
    for cut in cuts[1:]:
        factor_of = factor_of * one(*cut)
    return factor_of


def scatter_about(rng, dims, deviation, reach, split=(), dtype=jnp.bfloat16):
    values = jax.random.normal(rng, dims, jnp.float32) * deviation
    if len(split) > 0:
        values = level_of(rng, dims, split, -0.22, 0.18) * values
    return jnp.clip(values, min=-reach, max=reach).astype(dtype)


def setup_inputs(seed: int = 0, part: int = 0) -> dict:
    key_list = jax.random.split(jax.random.key(seed), 12)
    part_splits = jax.random.split(jax.random.fold_in(key_list[11], part), 12)
    return {
        "out_grad": scatter_about(part_splits[0], (D, LENGTH), 1.0, 6.0, ((1, 16),)),
        "gate_one": scatter_about(part_splits[1], (D, LENGTH), 1.0, 6.0, ((1, 16),)),
        "gate_two": scatter_about(part_splits[2], (D, LENGTH), 1.0, 6.0, ((1, 16),)),
        "conv_one": scatter_about(part_splits[3], (D, LENGTH), 1.0, 6.0, ((1, 16),)),
        "conv_two": scatter_about(part_splits[4], (D, LENGTH), 1.0, 6.0, ((1, 16),)),
        "value": scatter_about(part_splits[5], (D, LENGTH), 1.0, 6.0, ((1, 16),)),
        "filter_one": scatter_about(key_list[6], (D, LENGTH), 1.0, 6.0, ((0, 16),), jnp.float32),
        "filter_two": scatter_about(key_list[7], (D, LENGTH), 1.0, 6.0, ((0, 16),), jnp.float32),
        "skip_one": scatter_about(key_list[8], (D,), 1.0, 4.0, ((0, 16),), jnp.float32),
        "skip_two": scatter_about(key_list[9], (D,), 1.0, 4.0, ((0, 16),), jnp.float32),
        "short_weight": scatter_about(key_list[10], (D, KSHORT), KSHORT ** -0.5, 3.5, (), jnp.float32),
    }


def adjoint(grad, other, filt, skip):
    total = 2 * LENGTH
    scale = LENGTH ** -0.5
    block = math.gcd(D, 256)

    def one_block(items):
        grad_blk, other_blk, filt_blk, skip_blk = items
        spec_grad = jnp.fft.fft(grad_blk, n=total, axis=1)
        spec_filt = jnp.fft.fft(filt_blk * scale, n=total, axis=1)
        spec_other = jnp.fft.fft(other_blk, n=total, axis=1)
        back = jnp.real(jnp.fft.ifft(jnp.conj(spec_filt) * spec_grad, axis=1))[:, :LENGTH]
        back = back + skip_blk[:, None] * grad_blk
        filt_grad = jnp.real(jnp.fft.ifft(jnp.conj(spec_other) * spec_grad, axis=1))[:, :LENGTH] * scale
        return back, filt_grad

    count = D // block
    items = (grad.reshape(count, block, LENGTH), other.reshape(count, block, LENGTH),
             filt.reshape(count, block, LENGTH), skip.reshape(count, block))
    back, filt_grad = lax.map(one_block, items)
    return back.reshape(D, LENGTH), filt_grad.reshape(D, LENGTH)


def reference(out_grad, gate_one, gate_two, conv_one, conv_two, value, filter_one, filter_two, skip_one, skip_two, short_weight):
    f32 = jnp.float32
    bf16 = jnp.bfloat16
    gate_two_grad = (out_grad.astype(f32) * conv_two.astype(f32)).astype(bf16)
    conv_two_grad = (out_grad.astype(f32) * gate_two.astype(f32)).astype(bf16)
    inner = (gate_one.astype(f32) * conv_one.astype(f32)).astype(bf16)
    inner_grad_full, filter_two_grad = adjoint(conv_two_grad.astype(f32), inner.astype(f32), filter_two, skip_two)
    inner_grad = inner_grad_full.astype(bf16)
    gate_one_grad = (inner_grad.astype(f32) * conv_one.astype(f32)).astype(bf16)
    conv_one_grad = (inner_grad.astype(f32) * gate_one.astype(f32)).astype(bf16)
    value_grad_full, filter_one_grad = adjoint(conv_one_grad.astype(f32), value.astype(f32), filter_one, skip_one)
    value_grad = value_grad_full.astype(bf16)
    padded = jnp.pad(value_grad.astype(f32), ((0, 0), (0, KSHORT - 1)))
    proj_grad = jnp.zeros((D, LENGTH), f32)
    for offset in range(KSHORT):
        proj_grad = proj_grad + short_weight[:, offset:offset + 1] * padded[:, offset:offset + LENGTH]
    return proj_grad.astype(bf16), gate_one_grad, gate_two_grad, filter_one_grad, filter_two_grad
```

```python
import functools
import math

import jax
import jax.numpy as jnp
import numpy as np
from jax import lax
from jax.experimental import pallas as pl
from jax.experimental.pallas import tpu as pltpu
from jax.sharding import PartitionSpec as P

F32 = jnp.float32
BF16 = jnp.bfloat16
ROWS = 16


def cmul_const(x, angle, gain=1.0):
    re, im = x
    c, s = gain * math.cos(angle), gain * math.sin(angle)
    if abs(s) < 1e-12:
        if abs(c - 1.0) < 1e-12:
            return x
        return (re * c, im * c)
    if abs(c) < 1e-12:
        if abs(s + 1.0) < 1e-12:
            return (im, -re)
        if abs(s - 1.0) < 1e-12:
            return (-im, re)
    if abs(abs(c) - abs(s)) < 1e-12:
        m = abs(c)
        sc, ss = (1.0 if c > 0 else -1.0), (1.0 if s > 0 else -1.0)
        a = (re - im) if sc * ss > 0 else (re + im)
        b = (re + im) if sc * ss > 0 else (im - re)
        return (a * (m * sc), b * (m * sc))
    return (re * c - im * s, re * s + im * c)


def cdft(xs, sign):
    n = len(xs)
    if n == 1:
        return list(xs)
    even, odd = cdft(xs[0::2], sign), cdft(xs[1::2], sign)
    half = n // 2
    low, high = [], []
    for k in range(half):
        (er, ei), (tr, ti) = even[k], cmul_const(odd[k], sign * 2.0 * math.pi * k / n)
        low.append((er + tr, ei + ti))
        high.append((er - tr, ei - ti))
    return low + high


def odd_part(y, n):
    quarter = n // 4
    u = [cmul_const((y[j], -y[j + quarter]), -2.0 * math.pi * j / n) for j in range(quarter)]
    out = {}
    for p, (re, im) in enumerate(cdft(u, -1)):
        k = 4 * p + 1
        if k <= n // 2:
            out[k] = (re, im)
        else:
            out[n - k] = (re, -im)
    return out


def rdft(xs):
    n = len(xs)
    if n == 1:
        return [(xs[0], None)]
    half = n // 2
    even = rdft([xs[j] + xs[j + half] for j in range(half)])
    if n == 2:
        return [even[0], (xs[0] - xs[1], None)]
    odd = odd_part([xs[j] - xs[j + half] for j in range(half)], n)
    return [even[k // 2] if k % 2 == 0 else odd[k] for k in range(half + 1)]


def rdft_padded(xs):
    n = 2 * len(xs)
    even, odd = rdft(xs), odd_part(xs, n)
    return [even[k // 2] if k % 2 == 0 else odd[k] for k in range(len(xs) + 1)]


def odd_back(spec, n):
    quarter = n // 4
    u = []
    for p in range(quarter):
        k = 4 * p + 1
        if k <= n // 2:
            u.append(spec[k])
        else:
            re, im = spec[n - k]
            u.append((re, -im))
    v = cdft(u, 1)
    low, high = [], []
    for j in range(quarter):
        re, im = cmul_const(v[j], 2.0 * math.pi * j / n, 2.0)
        low.append(re)
        high.append(-im)
    return low + high


def irdft(spec):
    n = 2 * (len(spec) - 1)
    if n == 2:
        a, b = spec[0][0], spec[1][0]
        return [a + b, a - b]
    even, odd = irdft(spec[0::2]), odd_back(spec, n)
    return [e + o for e, o in zip(even, odd)] + [e - o for e, o in zip(even, odd)]


def irdft_half(spec):
    n = 2 * (len(spec) - 1)
    even, odd = irdft(spec[0::2]), odd_back(spec, n)
    return [e + o for e, o in zip(even, odd)]


def split(x):
    hi = x.astype(BF16)
    return hi, (x - hi.astype(F32)).astype(BF16)


def tables(blocks, width, scale):
    k1 = np.arange(blocks + 1, dtype=np.float64)[:, None]
    f = np.arange(width, dtype=np.float64)
    total = 2 * blocks * width
    angle = 2.0 * np.pi * (k1 * f[None, :]) / total
    twiddle = np.stack([np.cos(angle), -np.sin(angle)], axis=1).reshape(-1, width)
    theta = 2.0 * np.pi * ((f[:, None] * f[None, :]) % width) / width
    c, s = np.cos(theta), np.sin(theta)
    matrix = np.block([[c, -s], [s, c]]).astype(np.float32)
    hi = matrix.astype(jnp.bfloat16)
    lo = (matrix - hi.astype(np.float32)).astype(jnp.bfloat16)
    return hi, lo, twiddle.astype(np.float32), (twiddle * scale).astype(np.float32)


def row_tile(rows):
    best = ROWS
    for size in range(ROWS, 289, ROWS):
        if rows % size == 0:
            best = size
    return best


def spread(read, twiddle_ref, hi_ref, lo_ref, channels, blocks, width):
    def body(g, carry):
        start = pl.multiple_of(g * ROWS, ROWS)
        spec = rdft_padded([read(b, start) for b in range(blocks)])
        for k, (re, im) in enumerate(spec):
            c = twiddle_ref[2 * k : 2 * k + 1, :]
            s = twiddle_ref[2 * k + 1 : 2 * k + 2, :]
            if im is None:
                tr, ti = re * c, re * s
            else:
                tr, ti = re * c - im * s, re * s + im * c
            rows = pl.ds(pl.multiple_of(k * channels + start, ROWS), ROWS)
            for value, at in ((tr, 0), (ti, width)):
                hi, lo = split(value)
                hi_ref[rows, at : at + width] = hi
                lo_ref[rows, at : at + width] = lo
        return carry

    lax.fori_loop(0, channels // ROWS, body, 0)


def gather(spec_ref, twiddle_ref, start, channels, blocks, width):
    spec = []
    for k in range(blocks + 1):
        rows = pl.ds(pl.multiple_of(k * channels + start, ROWS), ROWS)
        re, im = spec_ref[rows, :width], spec_ref[rows, width:]
        c = twiddle_ref[2 * k : 2 * k + 1, :]
        s = twiddle_ref[2 * k + 1 : 2 * k + 2, :]
        if k == 0 or k == blocks:
            spec.append((re * c + im * s, None))
        else:
            spec.append((re * c + im * s, im * c - re * s))
    return irdft_half(spec)


def dot3(hi, lo, mat_hi, mat_lo, dims):
    def dot(a, b):
        return lax.dot_general(a, b, (dims, ((), ())), preferred_element_type=F32)

    return dot(hi, mat_hi) + dot(lo, mat_hi) + dot(hi, mat_lo)


FORWARD = ((1,), (0,))
BACK = ((1,), (1,))


def spectrum_kernel(channels, blocks, width, one_ref, two_ref, mat_hi, mat_lo, tw_ref,
                    out_one, out_two, hi_ref, lo_ref):
    rows = (blocks + 1) * channels
    tile = row_tile(rows)
    for filt, out in ((two_ref, out_two), (one_ref, out_one)):
        spread(lambda b, start: filt[pl.ds(start, ROWS), b * width : (b + 1) * width],
               tw_ref, hi_ref, lo_ref, channels, blocks, width)
        for at in range(0, rows, tile):
            out[at : at + tile, :] = dot3(
                hi_ref[at : at + tile, :], lo_ref[at : at + tile, :],
                mat_hi[...], mat_lo[...], FORWARD)


def multiply_back(spec, other, mat_hi, mat_lo, width):
    gr, gi = spec[:, :width], spec[:, width:]
    hr, hi = other[:, :width], other[:, width:]
    zr, zi = gr * hr + gi * hi, gi * hr - gr * hi
    z_hi, z_lo = split(jnp.concatenate([zr, zi], axis=1))
    return dot3(z_hi, z_lo, mat_hi[...], mat_lo[...], BACK)


def adjoint_kernel(channels, blocks, width, in_ref, h_two, h_one, skip_two, skip_one, taps_ref,
                   mat_hi, mat_lo, tw_ref, out_ref, spec_two, spec_one, hi_ref, lo_ref, back_ref,
                   grad_ref):
    rows = (blocks + 1) * channels
    tile = row_tile(rows)

    def convolve(h_ref, spec_ref):
        for at in range(0, rows, tile):
            here = slice(at, at + tile)
            spec = dot3(hi_ref[here, :], lo_ref[here, :], mat_hi[...], mat_lo[...], FORWARD)
            spec_ref[here, :] = spec
            back_ref[here, :] = multiply_back(spec, h_ref[here, :], mat_hi, mat_lo, width)

    spread(lambda b, start: in_ref[b, 0, pl.ds(start, ROWS), :].astype(F32),
           tw_ref, hi_ref, lo_ref, channels, blocks, width)
    convolve(h_two, spec_two)

    def first(g, carry):
        start = pl.multiple_of(g * ROWS, ROWS)
        here = pl.ds(start, ROWS)
        skip = skip_two[here, :]
        back = gather(back_ref, tw_ref, start, channels, blocks, width)
        for b in range(blocks):
            full = back[b] + skip * in_ref[b, 0, here, :].astype(F32)
            grad = full.astype(BF16)
            out_ref[b, 0, here, :] = grad
            grad_ref[b, here, :] = (grad.astype(F32) * in_ref[b, 1, here, :].astype(F32)).astype(BF16)
        return carry

    lax.fori_loop(0, channels // ROWS, first, 0)
    spread(lambda b, start: grad_ref[b, pl.ds(start, ROWS), :].astype(F32),
           tw_ref, hi_ref, lo_ref, channels, blocks, width)
    convolve(h_one, spec_one)
    lane = lax.broadcasted_iota(jnp.int32, (ROWS, width), 1)
    count = taps_ref.shape[1]

    def second(g, carry):
        start = pl.multiple_of(g * ROWS, ROWS)
        here = pl.ds(start, ROWS)
        skip = skip_one[here, :]
        back = gather(back_ref, tw_ref, start, channels, blocks, width)
        grads = []
        for b in range(blocks):
            full = back[b] + skip * grad_ref[b, here, :].astype(F32)
            grads.append(full.astype(BF16).astype(F32))
        grads.append(jnp.zeros((ROWS, width), F32))
        sums = [taps_ref[here, 0:1] * grads[b] for b in range(blocks)]
        for k in range(1, count):
            turned = [pltpu.roll(v, width - k, 1) for v in grads]
            for b in range(blocks):
                moved = jnp.where(lane < width - k, turned[b], turned[b + 1])
                sums[b] = sums[b] + taps_ref[here, k : k + 1] * moved
        for b in range(blocks):
            out_ref[b, 1, here, :] = sums[b].astype(BF16)
        return carry

    lax.fori_loop(0, channels // ROWS, second, 0)


def filter_kernel(channels, blocks, width, in_ref, spec_two, spec_one, mat_hi, mat_lo, tw_ref,
                  tw_scaled, out_one, out_two, hi_ref, lo_ref, back_ref):
    rows = (blocks + 1) * channels
    tile = row_tile(rows)
    for index, spec_ref, out in ((0, spec_two, out_two), (1, spec_one, out_one)):
        spread(lambda b, start: in_ref[b, index, pl.ds(start, ROWS), :].astype(F32),
               tw_scaled, hi_ref, lo_ref, channels, blocks, width)
        for at in range(0, rows, tile):
            here = slice(at, at + tile)
            other = dot3(hi_ref[here, :], lo_ref[here, :], mat_hi[...], mat_lo[...], FORWARD)
            back_ref[here, :] = multiply_back(spec_ref[here, :], other, mat_hi, mat_lo, width)

        def body(g, carry):
            start = pl.multiple_of(g * ROWS, ROWS)
            back = gather(back_ref, tw_ref, start, channels, blocks, width)
            for b in range(blocks):
                out[pl.ds(start, ROWS), b * width : (b + 1) * width] = back[b]
            return carry

        lax.fori_loop(0, channels // ROWS, body, 0)


def call(kernel, out_shape, scratch, flops, moved, *args):
    vmem = pl.BlockSpec(memory_space=pltpu.VMEM)
    return pl.pallas_call(
        kernel,
        out_shape=out_shape,
        in_specs=[vmem] * len(args),
        out_specs=[vmem] * len(out_shape),
        scratch_shapes=scratch,
        compiler_params=pltpu.CompilerParams(vmem_limit_bytes=44 * 1024 * 1024),
        cost_estimate=pl.CostEstimate(flops=flops, bytes_accessed=moved, transcendentals=0),
    )(*args)


def exchange(value):
    return lax.all_to_all(value, "seq", split_axis=0, concat_axis=0, tiled=True)


def local(
    out_grad,
    gate_one,
    gate_two,
    conv_one,
    conv_two,
    value,
    filter_one,
    filter_two,
    skip_one,
    skip_two,
    short_weight,
):
    blocks = lax.axis_size("seq")
    width = out_grad.shape[1]
    channels = filter_one.shape[0]
    length = filter_one.shape[1]
    rows = (blocks + 1) * channels
    shape = (blocks, channels, width)
    mat_hi, mat_lo, tw, tw_scaled = tables(
        blocks, width, length ** (-0.5) / (2 * length))
    work = 3 * 2 * rows * (2 * width) ** 2
    size = rows * 2 * width * 4

    def struct(*dims, dtype=F32):
        return jax.ShapeDtypeStruct(dims, dtype)

    def product(a, b):
        return (a.astype(F32) * b.astype(F32)).astype(BF16)

    halves = [pltpu.VMEM((rows, 2 * width), BF16), pltpu.VMEM((rows, 2 * width), BF16)]
    back = pltpu.VMEM((rows, 2 * width), F32)
    spec = struct(rows, 2 * width)

    cg_two = product(out_grad, gate_two).reshape(shape)
    first = exchange(jnp.stack([cg_two, gate_one.reshape(shape)], axis=1))
    inner = product(gate_one, conv_one).reshape(shape)
    second_in = jnp.stack([inner, value.reshape(shape)], axis=1)

    h_one, h_two = call(
        functools.partial(spectrum_kernel, channels, blocks, width),
        [spec, spec], halves, 2 * work, 4 * size,
        filter_one, filter_two, mat_hi, mat_lo, tw_scaled)
    second_in, first = lax.optimization_barrier((second_in, first))
    second = exchange(second_in)

    me = lax.axis_index("seq")
    taps = lax.dynamic_slice_in_dim(short_weight, me * channels, channels, axis=0)
    grads, spec_two, spec_one = call(
        functools.partial(adjoint_kernel, channels, blocks, width),
        [struct(blocks, 2, channels, width, dtype=BF16), spec, spec],
        halves + [back, pltpu.VMEM(shape, BF16)], 4 * work, 8 * size,
        first, h_two, h_one, skip_two[:, None], skip_one[:, None], taps, mat_hi, mat_lo, tw)
    grads, second = lax.optimization_barrier((grads, second))
    third = exchange(grads)

    filter_one_grad, filter_two_grad = call(
        functools.partial(filter_kernel, channels, blocks, width),
        [struct(channels, length), struct(channels, length)],
        halves + [back], 4 * work, 8 * size,
        second, spec_two, spec_one, mat_hi, mat_lo, tw, tw_scaled)
    gate_two_grad = product(out_grad, conv_two)
    inner_grad = third[:, 0].reshape(out_grad.shape)
    proj_grad = third[:, 1].reshape(out_grad.shape)
    gate_one_grad = product(inner_grad, conv_one)
    return (proj_grad, gate_one_grad, gate_two_grad, filter_one_grad, filter_two_grad)


def solution(mesh):
    frames = P(None, ("groups", "seq"))
    return jax.shard_map(
        local,
        mesh=mesh,
        in_specs=(frames,) * 6 + (P("seq", None),) * 2 + (P("seq"),) * 2 + (P(),),
        out_specs=(frames,) * 3 + (P(("groups", "seq"), None),) * 2,
        check_vma=False,
    )
```

```python
import functools
import math

import jax
import jax.numpy as jnp
import numpy as np
from jax import lax
from jax.experimental import pallas as pl
from jax.experimental.pallas import tpu as pltpu
from jax.sharding import PartitionSpec as P

F32 = jnp.float32
BF16 = jnp.bfloat16
ROWS = 16
SPARE = 6 * 1024 * 1024
WHOLE = 64128 * 1024
PARTS = 4
TILE = 272


def cmul_const(x, angle, gain=1.0):
    re, im = x
    c, s = gain * math.cos(angle), gain * math.sin(angle)
    if abs(s) < 1e-12:
        if abs(c - 1.0) < 1e-12:
            return x
        return (re * c, im * c)
    if abs(c) < 1e-12:
        if abs(s + 1.0) < 1e-12:
            return (im, -re)
        if abs(s - 1.0) < 1e-12:
            return (-im, re)
    if abs(abs(c) - abs(s)) < 1e-12:
        m = abs(c)
        sc, ss = (1.0 if c > 0 else -1.0), (1.0 if s > 0 else -1.0)
        a = (re - im) if sc * ss > 0 else (re + im)
        b = (re + im) if sc * ss > 0 else (im - re)
        return (a * (m * sc), b * (m * sc))
    return (re * c - im * s, re * s + im * c)


def cdft(xs, sign):
    n = len(xs)
    if n == 1:
        return list(xs)
    even, odd = cdft(xs[0::2], sign), cdft(xs[1::2], sign)
    half = n // 2
    low, high = [], []
    for k in range(half):
        (er, ei), (tr, ti) = even[k], cmul_const(odd[k], sign * 2.0 * math.pi * k / n)
        low.append((er + tr, ei + ti))
        high.append((er - tr, ei - ti))
    return low + high


def odd_part(y, n):
    quarter = n // 4
    u = [cmul_const((y[j], -y[j + quarter]), -2.0 * math.pi * j / n) for j in range(quarter)]
    out = {}
    for p, (re, im) in enumerate(cdft(u, -1)):
        k = 4 * p + 1
        if k <= n // 2:
            out[k] = (re, im)
        else:
            out[n - k] = (re, -im)
    return out


def rdft(xs):
    n = len(xs)
    if n == 1:
        return [(xs[0], None)]
    half = n // 2
    even = rdft([xs[j] + xs[j + half] for j in range(half)])
    if n == 2:
        return [even[0], (xs[0] - xs[1], None)]
    odd = odd_part([xs[j] - xs[j + half] for j in range(half)], n)
    return [even[k // 2] if k % 2 == 0 else odd[k] for k in range(half + 1)]


def rdft_padded(xs):
    n = 2 * len(xs)
    even, odd = rdft(xs), odd_part(xs, n)
    return [even[k // 2] if k % 2 == 0 else odd[k] for k in range(len(xs) + 1)]


def odd_back(spec, n):
    quarter = n // 4
    u = []
    for p in range(quarter):
        k = 4 * p + 1
        if k <= n // 2:
            u.append(spec[k])
        else:
            re, im = spec[n - k]
            u.append((re, -im))
    v = cdft(u, 1)
    low, high = [], []
    for j in range(quarter):
        re, im = cmul_const(v[j], 2.0 * math.pi * j / n, 2.0)
        low.append(re)
        high.append(-im)
    return low + high


def irdft(spec):
    n = 2 * (len(spec) - 1)
    if n == 2:
        a, b = spec[0][0], spec[1][0]
        return [a + b, a - b]
    even, odd = irdft(spec[0::2]), odd_back(spec, n)
    return [e + o for e, o in zip(even, odd)] + [e - o for e, o in zip(even, odd)]


def irdft_half(spec):
    n = 2 * (len(spec) - 1)
    even, odd = irdft(spec[0::2]), odd_back(spec, n)
    return [e + o for e, o in zip(even, odd)]


def split(x):
    hi = x.astype(BF16)
    return hi, (x - hi.astype(F32)).astype(BF16)


def tables(blocks, width, scale):
    k1 = np.arange(blocks + 1, dtype=np.float64)[:, None]
    f = np.arange(width, dtype=np.float64)
    total = 2 * blocks * width
    angle = 2.0 * np.pi * (k1 * f[None, :]) / total
    twiddle = np.stack([np.cos(angle), -np.sin(angle)], axis=1).reshape(-1, width)
    theta = 2.0 * np.pi * ((f[:, None] * f[None, :]) % width) / width
    c, s = np.cos(theta), np.sin(theta)
    matrix = np.block([[c, -s], [s, c]]).astype(np.float32)
    hi = matrix.astype(jnp.bfloat16)
    lo = (matrix - hi.astype(np.float32)).astype(jnp.bfloat16)
    return hi, lo, twiddle.astype(np.float32), (twiddle * scale).astype(np.float32)


def spread(xs, twiddle_ref, hi_ref, lo_ref):
    width = xs[0].shape[1]
    for k, (re, im) in enumerate(rdft_padded(xs)):
        c = twiddle_ref[2 * k : 2 * k + 1, :]
        s = twiddle_ref[2 * k + 1 : 2 * k + 2, :]
        if im is None:
            tr, ti = re * c, re * s
        else:
            tr, ti = re * c - im * s, re * s + im * c
        for value, at in ((tr, 0), (ti, width)):
            hi, lo = split(value)
            hi_ref[k * ROWS : (k + 1) * ROWS, at : at + width] = hi
            lo_ref[k * ROWS : (k + 1) * ROWS, at : at + width] = lo


def gather(spec_ref, twiddle_ref, width):
    spec = []
    last = spec_ref.shape[0] // ROWS - 1
    for k in range(last + 1):
        rows = slice(k * ROWS, (k + 1) * ROWS)
        re, im = spec_ref[rows, :width], spec_ref[rows, width:]
        c = twiddle_ref[2 * k : 2 * k + 1, :]
        s = twiddle_ref[2 * k + 1 : 2 * k + 2, :]
        if k == 0 or k == last:
            spec.append((re * c + im * s, None))
        else:
            spec.append((re * c + im * s, im * c - re * s))
    return irdft_half(spec)


def dot3(hi, lo, mat_hi, mat_lo, dims):
    def dot(a, b):
        return lax.dot_general(a, b, (dims, ((), ())), preferred_element_type=F32)

    return dot(hi, mat_hi) + dot(lo, mat_hi) + dot(hi, mat_lo)


FORWARD = ((1,), (0,))
BACK = ((1,), (1,))


def tiles(rows):
    size = TILE if rows % TILE == 0 else rows
    return [slice(at, at + size) for at in range(0, rows, size)]


def multiply_back(spec, other, mat_hi, mat_lo, width):
    gr, gi = spec[:, :width], spec[:, width:]
    hr, hi = other[:, :width], other[:, width:]
    zr, zi = gr * hr + gi * hi, gi * hr - gr * hi
    z_hi, z_lo = split(jnp.concatenate([zr, zi], axis=1))
    return dot3(z_hi, z_lo, mat_hi[...], mat_lo[...], BACK)


def staggered(groups, stages):
    for t in range(groups + len(stages) - 1):
        for s in reversed(range(len(stages))):
            if 0 <= t - s < groups:
                stages[s](t - s)


def spectrum_kernel(blocks, width, one_ref, two_ref, mat_hi, mat_lo, tw_ref, out_one, out_two,
                    hi_ref, lo_ref):
    groups = one_ref.shape[0] // ROWS

    def source(g):
        refs = (two_ref, out_two) if g < groups else (one_ref, out_one)
        return refs + (g % groups,)

    def load(g):
        filt, _, at = source(g)
        rows = slice(at * ROWS, (at + 1) * ROWS)
        xs = [filt[rows, b * width : (b + 1) * width] for b in range(blocks)]
        spread(xs, tw_ref, hi_ref.at[g % 2], lo_ref.at[g % 2])

    def transform(g):
        _, out, at = source(g)
        for here in tiles(hi_ref.shape[1]):
            out[at, here, :] = dot3(hi_ref[g % 2, here, :], lo_ref[g % 2, here, :], mat_hi[...],
                                    mat_lo[...], FORWARD)

    staggered(2 * groups, [load, transform])


def adjoint_kernel(blocks, width, sent, filt_two, filt_one, skip_two, skip_one, taps_ref,
                   mat_hi, mat_lo, tw_ref, back_far, grad_far,
                   hi_two, lo_two, back_two, hi_one, lo_one, back_one,
                   in_ref, h_two, h_one, out_ref, grad_ref, sems):
    groups = h_two.shape[0]
    parts = math.gcd(groups, PARTS)
    each = groups // parts

    def moves(part):
        some = pl.ds(part * each, each)
        rows = pl.ds(part * each * ROWS, each * ROWS)
        pairs = (
            (sent.at[:, pl.ds(0, 2), rows, :], in_ref.at[:, :, rows, :]),
            (filt_two.at[some], h_two.at[some]),
            (filt_one.at[some], h_one.at[some]),
            (grad_ref.at[:, rows, :], grad_far.at[:, rows, :]),
            (out_ref.at[:, 0, rows, :], back_far.at[:, 0, rows, :]),
            (out_ref.at[:, 1, rows, :], back_far.at[:, 1, rows, :]),
        )
        return [pltpu.make_async_copy(source, target, sems.at[part * len(pairs) + i])
                for i, (source, target) in enumerate(pairs)]

    copies = [moves(part) for part in range(parts)]
    for index in (0, 1, 2):
        for copy in copies:
            copy[index].start()

    def begin(g, index):
        if g == 0:
            for copy in copies:
                copy[index].wait()

    def end(g, index):
        if g == groups - 1:
            for copy in copies:
                copy[index].start()

    lane = lax.broadcasted_iota(jnp.int32, (ROWS, width), 1)
    count = taps_ref.shape[1]

    def rows_of(g):
        return slice(g * ROWS, (g + 1) * ROWS)

    def convolve(g, h_ref, hi_ref, lo_ref, back_ref):
        p = g % 2
        for here in tiles(hi_ref.shape[1]):
            spec = dot3(hi_ref[p, here, :], lo_ref[p, here, :], mat_hi[...], mat_lo[...], FORWARD)
            back_ref[p, here, :] = multiply_back(spec, h_ref[g, here, :], mat_hi, mat_lo, width)

    def load(g):
        begin(g, 0)
        here = rows_of(g)
        xs = [in_ref[b, 0, here, :].astype(F32) for b in range(blocks)]
        spread(xs, tw_ref, hi_two.at[g % 2], lo_two.at[g % 2])

    def first(g):
        begin(g, 1)
        convolve(g, h_two, hi_two, lo_two, back_two)

    def between(g):
        here = rows_of(g)
        skip = skip_two[here, :]
        back = gather(back_two.at[g % 2], tw_ref, width)
        grads = []
        for b in range(blocks):
            full = back[b] + skip * in_ref[b, 0, here, :].astype(F32)
            grad = full.astype(BF16)
            out_ref[b, 0, here, :] = grad
            grad = (grad.astype(F32) * in_ref[b, 1, here, :].astype(F32)).astype(BF16)
            grad_ref[b, here, :] = grad
            grads.append(grad.astype(F32))
        end(g, 3)
        end(g, 4)
        spread(grads, tw_ref, hi_one.at[g % 2], lo_one.at[g % 2])

    def second(g):
        begin(g, 2)
        convolve(g, h_one, hi_one, lo_one, back_one)

    def finish(g):
        here = rows_of(g)
        skip = skip_one[here, :]
        back = gather(back_one.at[g % 2], tw_ref, width)
        grads = []
        for b in range(blocks):
            full = back[b] + skip * grad_ref[b, here, :].astype(F32)
            grads.append(full.astype(BF16).astype(F32))
        grads.append(jnp.zeros((ROWS, width), F32))
        sums = [taps_ref[here, 0:1] * grads[b] for b in range(blocks)]
        for k in range(1, count):
            turned = [pltpu.roll(v, width - k, 1) for v in grads]
            for b in range(blocks):
                moved = jnp.where(lane < width - k, turned[b], turned[b + 1])
                sums[b] = sums[b] + taps_ref[here, k : k + 1] * moved
        for b in range(blocks):
            out_ref[b, 1, here, :] = sums[b].astype(BF16)
        end(g, 5)

    staggered(groups, [load, first, between, second, finish])
    for copy in copies:
        for index in (3, 4, 5):
            copy[index].wait()


def filter_kernel(blocks, width, me_ref, in_ref, inner_ref, grad_ref, mat_hi, mat_lo, tw_ref, tw_scaled,
                  out_one, out_two, hi_ref, lo_ref, other_hi, other_lo, back_ref):
    groups = grad_ref.shape[1] // ROWS
    me = me_ref[0]

    def load(g):
        p = g % 2
        rows = slice((g % groups) * ROWS, (g % groups + 1) * ROWS)
        if g < groups:
            xs = [in_ref[b, 2, rows, :].astype(F32) for b in range(blocks)]
            grads = [grad_ref[b, rows, :].astype(F32) for b in range(blocks)]
        else:
            xs = [inner_ref[me ^ b, rows, :].astype(F32) for b in range(blocks)]
            grads = [in_ref[b, 0, rows, :].astype(F32) for b in range(blocks)]
        spread(xs, tw_scaled, other_hi.at[p], other_lo.at[p])
        spread(grads, tw_ref, hi_ref.at[p], lo_ref.at[p])

    def transform(g):
        p = g % 2
        for here in tiles(hi_ref.shape[1]):
            spec = dot3(hi_ref[p, here, :], lo_ref[p, here, :], mat_hi[...], mat_lo[...], FORWARD)
            other = dot3(other_hi[p, here, :], other_lo[p, here, :], mat_hi[...], mat_lo[...],
                         FORWARD)
            back_ref[p, here, :] = multiply_back(spec, other, mat_hi, mat_lo, width)

    def finish(g):
        out = out_one if g < groups else out_two
        rows = slice((g % groups) * ROWS, (g % groups + 1) * ROWS)
        back = gather(back_ref.at[g % 2], tw_ref, width)
        for b in range(blocks):
            out[rows, b * width : (b + 1) * width] = back[b]

    staggered(2 * groups, [load, transform, finish])


def product(a, b):
    return (a.astype(F32) * b.astype(F32)).astype(BF16)


def send_kernel(out_grad, gate_two, gate_one, value, out, *refs):
    held, made, sems = refs[:4], refs[4], refs[5]
    blocks = out_grad.shape[0]
    parts = math.gcd(blocks, PARTS)
    step = blocks // parts
    arrive, leave = [], []
    for part in range(parts):
        here = pl.ds(part * step, step)
        arrive.append([pltpu.make_async_copy(ref.at[here], to.at[here], sems.at[7 * part + i])
                       for i, (ref, to) in enumerate(zip((out_grad, gate_two, gate_one, value), held))])
        leave.append([pltpu.make_async_copy(ref.at[here], out.at[here, i],
                                            sems.at[7 * part + 4 + i])
                      for i, ref in enumerate((made, held[2], held[3]))])
    for copies in arrive:
        for copy in copies:
            copy.start()
    for part in range(parts):
        here = slice(part * step, (part + 1) * step)
        for i in (2, 3):
            arrive[part][i].wait()
            leave[part][i - 1].start()
        for i in (0, 1):
            arrive[part][i].wait()
        made[here] = product(held[0][here], held[1][here])
        leave[part][0].start()
    for copies in leave:
        for copy in copies:
            copy.wait()


def receive_kernel(came, conv_one, proj_grad, gate_one_grad, made, sems):
    blocks = conv_one.shape[0]
    parts = math.gcd(blocks, PARTS)
    step = blocks // parts
    copies = [pltpu.make_async_copy(came.at[:, 1], proj_grad, sems.at[parts])]
    copies[0].start()
    for part in range(parts):
        here = pl.ds(part * step, step)
        made[here] = product(came[here, 0], conv_one[here])
        copies.append(pltpu.make_async_copy(made.at[here], gate_one_grad.at[here], sems.at[part]))
        copies[-1].start()
    for copy in copies:
        copy.wait()


def call(kernel, out_shape, scratch, flops, moved, *args, far=(), far_out=False, copies=0,
         limit=0):
    vmem = pl.BlockSpec(memory_space=pltpu.VMEM)
    smem = pl.BlockSpec(memory_space=pltpu.SMEM)
    hbm = pl.BlockSpec(memory_space=pltpu.HBM)
    held = sum(math.prod(dims) * np.dtype(dtype).itemsize for dims, dtype in scratch)
    buffers = [pltpu.VMEM(dims, dtype) for dims, dtype in scratch]
    if copies:
        buffers.append(pltpu.SemaphoreType.DMA((copies,)))
    return pl.pallas_call(
        kernel,
        out_shape=out_shape,
        in_specs=[smem if a.dtype == jnp.int32 else hbm if i in far else vmem
                  for i, a in enumerate(args)],
        out_specs=[hbm if far_out else vmem] * len(out_shape),
        scratch_shapes=buffers,
        compiler_params=pltpu.CompilerParams(
            vmem_limit_bytes=limit or held + SPARE),
        cost_estimate=pl.CostEstimate(flops=flops, bytes_accessed=moved, transcendentals=0),
    )(*args)


def exchange(value):
    return lax.all_to_all(value, "seq", split_axis=0, concat_axis=0, tiled=True)


def swap(value, step):
    count = lax.axis_size("seq")
    return lax.ppermute(value, "seq", [(j, j ^ step) for j in range(count)])


def exchange_near(value):
    me = lax.axis_index("seq")
    half = value.shape[0] // 2
    value = value.reshape((2, half) + value.shape[1:])
    mine = me // half
    value = jnp.concatenate(
        [lax.dynamic_index_in_dim(value, mine, 0), lax.dynamic_index_in_dim(value, 1 - mine, 0)])
    parts = [lax.dynamic_index_in_dim(value, (me % half) ^ r, 1) for r in range(half)]
    parts = lax.optimization_barrier(tuple(parts))
    came = [parts[0]] + [swap(parts[r], r) for r in range(1, half)]
    return ([part[0] for part in came], jnp.concatenate([part[1] for part in came]))


def local(
    out_grad,
    gate_one,
    gate_two,
    conv_one,
    conv_two,
    value,
    filter_one,
    filter_two,
    skip_one,
    skip_two,
    short_weight,
):
    blocks = lax.axis_size("seq")
    width = out_grad.shape[1]
    channels = filter_one.shape[0]
    length = filter_one.shape[1]
    rows = (blocks + 1) * channels
    shape = (blocks, channels, width)
    mat_hi, mat_lo, tw, tw_scaled = tables(
        blocks, width, length ** (-0.5) / (2 * length))
    work = 3 * 2 * rows * (2 * width) ** 2
    size = rows * 2 * width * 4

    def struct(*dims, dtype=F32):
        return jax.ShapeDtypeStruct(dims, dtype)

    groups = channels // ROWS
    tile = ((blocks + 1) * ROWS, 2 * width)
    halves = [((2,) + tile, BF16)] * 2
    back = ((2,) + tile, F32)
    spec = struct(groups, *tile)

    me = lax.axis_index("seq")
    taps = lax.dynamic_slice_in_dim(short_weight, me * channels, channels, axis=0)
    pair = struct(blocks, 2, channels, width, dtype=BF16)
    parts = math.gcd(blocks, PARTS)
    one = struct(*shape, dtype=BF16)
    triple = struct(blocks, 3, channels, width, dtype=BF16)
    first = exchange(call(
        send_kernel, [triple], [(shape, BF16)] * 5, 3 * pair.size, 7 * pair.size,
        *(a.reshape(shape) for a in (out_grad, gate_two, gate_one, value)),
        far=range(4), far_out=True, copies=7 * parts, limit=WHOLE)[0])
    near, far = exchange_near(product(gate_one, conv_one).reshape(shape))
    h_one, h_two = call(
        functools.partial(spectrum_kernel, blocks, width),
        [spec, spec], halves, 2 * work, 4 * size,
        filter_one, filter_two, mat_hi, mat_lo, tw_scaled)
    gate_two_grad = product(out_grad, conv_two)
    far = swap(far, blocks // 2)
    first, h_one, h_two, gate_two_grad = lax.optimization_barrier(
        (first, h_one, h_two, gate_two_grad))
    grads, cg_one = call(
        functools.partial(adjoint_kernel, blocks, width),
        [pair, struct(*shape, dtype=BF16)],
        (halves + [back]) * 2 + [(pair.shape, BF16)] + [((groups,) + tile, F32)] * 2
        + [(pair.shape, BF16), (shape, BF16)],
        4 * work, 8 * size,
        first, h_two, h_one, skip_two[:, None], skip_one[:, None], taps, mat_hi, mat_lo, tw,
        far=(0, 1, 2), far_out=True, copies=6 * math.gcd(groups, PARTS), limit=WHOLE)
    grads, far = lax.optimization_barrier((grads, far))
    inner = jnp.concatenate(near + [far])
    third = exchange(grads)
    filter_one_grad, filter_two_grad = call(
        functools.partial(filter_kernel, blocks, width),
        [struct(channels, length), struct(channels, length)],
        halves * 2 + [back], 6 * work, 8 * size,
        me[None].astype(jnp.int32), first, inner, cg_one, mat_hi, mat_lo, tw, tw_scaled)
    proj_grad, gate_one_grad = call(
        receive_kernel, [one, one], [(shape, BF16)], pair.size, 6 * pair.size,
        third, conv_one.reshape(shape), far_out=True, copies=parts + 1)
    proj_grad = proj_grad.reshape(out_grad.shape)
    gate_one_grad = gate_one_grad.reshape(out_grad.shape)
    return (proj_grad, gate_one_grad, gate_two_grad, filter_one_grad, filter_two_grad)


def solution(mesh):
    frames = P(None, ("groups", "seq"))
    return jax.shard_map(
        local,
        mesh=mesh,
        in_specs=(frames,) * 6 + (P("seq", None),) * 2 + (P("seq"),) * 2 + (P(),),
        out_specs=(frames,) * 3 + (P(("groups", "seq"), None),) * 2,
        check_vma=False,
    )
```

```python
import functools
import math

import jax
import jax.numpy as jnp
import numpy as np
from jax import lax
from jax.experimental import pallas as pl
from jax.experimental.pallas import tpu as pltpu
from jax.sharding import PartitionSpec as P

F32 = jnp.float32
BF16 = jnp.bfloat16
ROWS = 16
SPARE = 6 * 1024 * 1024
WHOLE = 64128 * 1024
PARTS = 4
TILE = 272


def cmul_const(x, angle, gain=1.0):
    re, im = x
    c, s = gain * math.cos(angle), gain * math.sin(angle)
    if abs(s) < 1e-12:
        if abs(c - 1.0) < 1e-12:
            return x
        return (re * c, im * c)
    if abs(c) < 1e-12:
        if abs(s + 1.0) < 1e-12:
            return (im, -re)
        if abs(s - 1.0) < 1e-12:
            return (-im, re)
    if abs(abs(c) - abs(s)) < 1e-12:
        m = abs(c)
        sc, ss = (1.0 if c > 0 else -1.0), (1.0 if s > 0 else -1.0)
        a = (re - im) if sc * ss > 0 else (re + im)
        b = (re + im) if sc * ss > 0 else (im - re)
        return (a * (m * sc), b * (m * sc))
    return (re * c - im * s, re * s + im * c)


def cdft(xs, sign):
    n = len(xs)
    if n == 1:
        return list(xs)
    even, odd = cdft(xs[0::2], sign), cdft(xs[1::2], sign)
    half = n // 2
    low, high = [], []
    for k in range(half):
        (er, ei), (tr, ti) = even[k], cmul_const(odd[k], sign * 2.0 * math.pi * k / n)
        low.append((er + tr, ei + ti))
        high.append((er - tr, ei - ti))
    return low + high


def odd_part(y, n):
    quarter = n // 4
    u = [cmul_const((y[j], -y[j + quarter]), -2.0 * math.pi * j / n) for j in range(quarter)]
    out = {}
    for p, (re, im) in enumerate(cdft(u, -1)):
        k = 4 * p + 1
        if k <= n // 2:
            out[k] = (re, im)
        else:
            out[n - k] = (re, -im)
    return out


def rdft(xs):
    n = len(xs)
    if n == 1:
        return [(xs[0], None)]
    half = n // 2
    even = rdft([xs[j] + xs[j + half] for j in range(half)])
    if n == 2:
        return [even[0], (xs[0] - xs[1], None)]
    odd = odd_part([xs[j] - xs[j + half] for j in range(half)], n)
    return [even[k // 2] if k % 2 == 0 else odd[k] for k in range(half + 1)]


def rdft_padded(xs):
    n = 2 * len(xs)
    even, odd = rdft(xs), odd_part(xs, n)
    return [even[k // 2] if k % 2 == 0 else odd[k] for k in range(len(xs) + 1)]


def odd_back(spec, n):
    quarter = n // 4
    u = []
    for p in range(quarter):
        k = 4 * p + 1
        if k <= n // 2:
            u.append(spec[k])
        else:
            re, im = spec[n - k]
            u.append((re, -im))
    v = cdft(u, 1)
    low, high = [], []
    for j in range(quarter):
        re, im = cmul_const(v[j], 2.0 * math.pi * j / n, 2.0)
        low.append(re)
        high.append(-im)
    return low + high


def irdft(spec):
    n = 2 * (len(spec) - 1)
    if n == 2:
        a, b = spec[0][0], spec[1][0]
        return [a + b, a - b]
    even, odd = irdft(spec[0::2]), odd_back(spec, n)
    return [e + o for e, o in zip(even, odd)] + [e - o for e, o in zip(even, odd)]


def irdft_half(spec):
    n = 2 * (len(spec) - 1)
    even, odd = irdft(spec[0::2]), odd_back(spec, n)
    return [e + o for e, o in zip(even, odd)]


def split(x):
    hi = x.astype(BF16)
    return hi, (x - hi.astype(F32)).astype(BF16)


def tables(blocks, width, scale):
    k1 = np.arange(blocks + 1, dtype=np.float64)[:, None]
    f = np.arange(width, dtype=np.float64)
    total = 2 * blocks * width
    angle = 2.0 * np.pi * (k1 * f[None, :]) / total
    twiddle = np.stack([np.cos(angle), -np.sin(angle)], axis=1).reshape(-1, width)
    theta = 2.0 * np.pi * ((f[:, None] * f[None, :]) % width) / width
    c, s = np.cos(theta), np.sin(theta)
    matrix = np.block([[c, -s], [s, c]]).astype(np.float32)
    hi = matrix.astype(jnp.bfloat16)
    lo = (matrix - hi.astype(np.float32)).astype(jnp.bfloat16)
    return hi, lo, twiddle.astype(np.float32), (twiddle * scale).astype(np.float32)


def spread(xs, twiddle_ref, hi_ref, lo_ref):
    width = xs[0].shape[1]
    for k, (re, im) in enumerate(rdft_padded(xs)):
        c = twiddle_ref[2 * k : 2 * k + 1, :]
        s = twiddle_ref[2 * k + 1 : 2 * k + 2, :]
        if im is None:
            tr, ti = re * c, re * s
        else:
            tr, ti = re * c - im * s, re * s + im * c
        for value, at in ((tr, 0), (ti, width)):
            hi, lo = split(value)
            hi_ref[k * ROWS : (k + 1) * ROWS, at : at + width] = hi
            lo_ref[k * ROWS : (k + 1) * ROWS, at : at + width] = lo


def gather(spec_ref, twiddle_ref, width):
    spec = []
    last = spec_ref.shape[0] // ROWS - 1
    for k in range(last + 1):
        rows = slice(k * ROWS, (k + 1) * ROWS)
        re, im = spec_ref[rows, :width], spec_ref[rows, width:]
        c = twiddle_ref[2 * k : 2 * k + 1, :]
        s = twiddle_ref[2 * k + 1 : 2 * k + 2, :]
        if k == 0 or k == last:
            spec.append((re * c + im * s, None))
        else:
            spec.append((re * c + im * s, im * c - re * s))
    return irdft_half(spec)


def dot3(hi, lo, mat_hi, mat_lo, dims):
    def dot(a, b):
        return lax.dot_general(a, b, (dims, ((), ())), preferred_element_type=F32)

    return dot(hi, mat_hi) + dot(lo, mat_hi) + dot(hi, mat_lo)


FORWARD = ((1,), (0,))
BACK = ((1,), (1,))


def tiles(rows):
    size = TILE if rows % TILE == 0 else rows
    return [slice(at, at + size) for at in range(0, rows, size)]


def multiply_back(spec, other, mat_hi, mat_lo, width):
    gr, gi = spec[:, :width], spec[:, width:]
    hr, hi = other[:, :width], other[:, width:]
    zr, zi = gr * hr + gi * hi, gi * hr - gr * hi
    z_hi, z_lo = split(jnp.concatenate([zr, zi], axis=1))
    return dot3(z_hi, z_lo, mat_hi[...], mat_lo[...], BACK)


def staggered(groups, stages):
    for t in range(groups + len(stages) - 1):
        for s in reversed(range(len(stages))):
            if 0 <= t - s < groups:
                stages[s](t - s)


def spectrum_kernel(blocks, width, one_ref, two_ref, mat_hi, mat_lo, tw_ref, out_one, out_two,
                    hi_ref, lo_ref):
    groups = one_ref.shape[0] // ROWS

    def source(g):
        refs = (two_ref, out_two) if g < groups else (one_ref, out_one)
        return refs + (g % groups,)

    def load(g):
        filt, _, at = source(g)
        rows = slice(at * ROWS, (at + 1) * ROWS)
        xs = [filt[rows, b * width : (b + 1) * width] for b in range(blocks)]
        spread(xs, tw_ref, hi_ref.at[g % 2], lo_ref.at[g % 2])

    def transform(g):
        _, out, at = source(g)
        for here in tiles(hi_ref.shape[1]):
            out[at, here, :] = dot3(hi_ref[g % 2, here, :], lo_ref[g % 2, here, :], mat_hi[...],
                                    mat_lo[...], FORWARD)

    staggered(2 * groups, [load, transform])


def adjoint_kernel(blocks, width, sent, filt_two, filt_one, skip_two, skip_one, taps_ref,
                   mat_hi, mat_lo, tw_ref, back_far, grad_far,
                   hi_two, lo_two, back_two, hi_one, lo_one, back_one,
                   in_ref, h_two, h_one, out_ref, grad_ref, sems):
    groups = h_two.shape[0]
    parts = math.gcd(groups, PARTS)
    each = groups // parts

    def moves(part):
        some = pl.ds(part * each, each)
        rows = pl.ds(part * each * ROWS, each * ROWS)
        pairs = (
            (sent.at[:, pl.ds(0, 2), rows, :], in_ref.at[:, :, rows, :]),
            (filt_two.at[some], h_two.at[some]),
            (filt_one.at[some], h_one.at[some]),
            (grad_ref.at[:, rows, :], grad_far.at[:, rows, :]),
            (out_ref.at[:, 0, rows, :], back_far.at[:, 0, rows, :]),
            (out_ref.at[:, 1, rows, :], back_far.at[:, 1, rows, :]),
        )
        return [pltpu.make_async_copy(source, target, sems.at[part * len(pairs) + i])
                for i, (source, target) in enumerate(pairs)]

    copies = [moves(part) for part in range(parts)]
    for index in (0, 1, 2):
        for copy in copies:
            copy[index].start()

    def begin(g, index):
        if g == 0:
            for copy in copies:
                copy[index].wait()

    def end(g, index):
        if g == groups - 1:
            for copy in copies:
                copy[index].start()

    lane = lax.broadcasted_iota(jnp.int32, (ROWS, width), 1)
    count = taps_ref.shape[1]

    def rows_of(g):
        return slice(g * ROWS, (g + 1) * ROWS)

    def convolve(g, h_ref, hi_ref, lo_ref, back_ref):
        p = g % 2
        for here in tiles(hi_ref.shape[1]):
            spec = dot3(hi_ref[p, here, :], lo_ref[p, here, :], mat_hi[...], mat_lo[...], FORWARD)
            back_ref[p, here, :] = multiply_back(spec, h_ref[g, here, :], mat_hi, mat_lo, width)

    def load(g):
        begin(g, 0)
        here = rows_of(g)
        xs = [in_ref[b, 0, here, :].astype(F32) for b in range(blocks)]
        spread(xs, tw_ref, hi_two.at[g % 2], lo_two.at[g % 2])

    def first(g):
        begin(g, 1)
        convolve(g, h_two, hi_two, lo_two, back_two)

    def between(g):
        here = rows_of(g)
        skip = skip_two[here, :]
        back = gather(back_two.at[g % 2], tw_ref, width)
        grads = []
        for b in range(blocks):
            full = back[b] + skip * in_ref[b, 0, here, :].astype(F32)
            grad = full.astype(BF16)
            out_ref[b, 0, here, :] = grad
            grad = (grad.astype(F32) * in_ref[b, 1, here, :].astype(F32)).astype(BF16)
            grad_ref[b, here, :] = grad
            grads.append(grad.astype(F32))
        end(g, 3)
        end(g, 4)
        spread(grads, tw_ref, hi_one.at[g % 2], lo_one.at[g % 2])

    def second(g):
        begin(g, 2)
        convolve(g, h_one, hi_one, lo_one, back_one)

    def finish(g):
        here = rows_of(g)
        skip = skip_one[here, :]
        back = gather(back_one.at[g % 2], tw_ref, width)
        grads = []
        for b in range(blocks):
            full = back[b] + skip * grad_ref[b, here, :].astype(F32)
            grads.append(full.astype(BF16).astype(F32))
        grads.append(jnp.zeros((ROWS, width), F32))
        sums = [taps_ref[here, 0:1] * grads[b] for b in range(blocks)]
        for k in range(1, count):
            turned = [pltpu.roll(v, width - k, 1) for v in grads]
            for b in range(blocks):
                moved = jnp.where(lane < width - k, turned[b], turned[b + 1])
                sums[b] = sums[b] + taps_ref[here, k : k + 1] * moved
        for b in range(blocks):
            out_ref[b, 1, here, :] = sums[b].astype(BF16)
        end(g, 5)

    staggered(groups, [load, first, between, second, finish])
    for copy in copies:
        for index in (3, 4, 5):
            copy[index].wait()


def filter_kernel(blocks, width, me_ref, in_ref, inner_ref, grad_ref, mat_hi, mat_lo, tw_ref, tw_scaled,
                  out_one, out_two, hi_ref, lo_ref, other_hi, other_lo, back_ref):
    groups = grad_ref.shape[1] // ROWS
    me = me_ref[0]

    def load(g):
        p = g % 2
        rows = slice((g % groups) * ROWS, (g % groups + 1) * ROWS)
        if g < groups:
            xs = [in_ref[b, 2, rows, :].astype(F32) for b in range(blocks)]
            grads = [grad_ref[b, rows, :].astype(F32) for b in range(blocks)]
        else:
            xs = [inner_ref[me ^ b, rows, :].astype(F32) for b in range(blocks)]
            grads = [in_ref[b, 0, rows, :].astype(F32) for b in range(blocks)]
        spread(xs, tw_scaled, other_hi.at[p], other_lo.at[p])
        spread(grads, tw_ref, hi_ref.at[p], lo_ref.at[p])

    def transform(g):
        p = g % 2
        for here in tiles(hi_ref.shape[1]):
            spec = dot3(hi_ref[p, here, :], lo_ref[p, here, :], mat_hi[...], mat_lo[...], FORWARD)
            other = dot3(other_hi[p, here, :], other_lo[p, here, :], mat_hi[...], mat_lo[...],
                         FORWARD)
            back_ref[p, here, :] = multiply_back(spec, other, mat_hi, mat_lo, width)

    def finish(g):
        out = out_one if g < groups else out_two
        rows = slice((g % groups) * ROWS, (g % groups + 1) * ROWS)
        back = gather(back_ref.at[g % 2], tw_ref, width)
        for b in range(blocks):
            out[rows, b * width : (b + 1) * width] = back[b]

    staggered(2 * groups, [load, transform, finish])


def product(a, b):
    return (a.astype(F32) * b.astype(F32)).astype(BF16)


def send_kernel(out_grad, gate_two, gate_one, value, out, *refs):
    held, made, sems = refs[:4], refs[4], refs[5]
    blocks = out_grad.shape[0]
    parts = math.gcd(blocks, PARTS)
    step = blocks // parts
    arrive, leave = [], []
    for part in range(parts):
        here = pl.ds(part * step, step)
        arrive.append([pltpu.make_async_copy(ref.at[here], to.at[here], sems.at[7 * part + i])
                       for i, (ref, to) in enumerate(zip((out_grad, gate_two, gate_one, value), held))])
        leave.append([pltpu.make_async_copy(ref.at[here], out.at[here, i],
                                            sems.at[7 * part + 4 + i])
                      for i, ref in enumerate((made, held[2], held[3]))])
    for copies in arrive:
        for copy in copies:
            copy.start()
    for part in range(parts):
        here = slice(part * step, (part + 1) * step)
        for i in (2, 3):
            arrive[part][i].wait()
            leave[part][i - 1].start()
        for i in (0, 1):
            arrive[part][i].wait()
        made[here] = product(held[0][here], held[1][here])
        leave[part][0].start()
    for copies in leave:
        for copy in copies:
            copy.wait()


def pairs_kernel(me_ref, gate_one, conv_one, *refs):
    *outs, gate, conv, made, sems = refs
    half = len(outs)
    me = me_ref[0]
    arrive = [pltpu.make_async_copy(ref, to, sems.at[half + i])
              for i, (ref, to) in enumerate(((gate_one, gate), (conv_one, conv)))]
    leave = [pltpu.make_async_copy(made.at[r], out, sems.at[r]) for r, out in enumerate(outs)]
    for copy in arrive:
        copy.start()
    for copy in arrive:
        copy.wait()
    for r in range(half):
        for i, index in enumerate((me ^ r, me ^ r ^ (half + half // 2))):
            made[r, i] = product(gate[index], conv[index])
        leave[r].start()
    for copy in leave:
        copy.wait()


def join_kernel(*refs):
    *parts, out, held, sems = refs
    half = len(parts)
    copies = [pltpu.make_async_copy(parts[r ^ (half // 2)].at[1], held.at[r], sems.at[r])
              for r in range(half)]
    for copy in copies:
        copy.start()
    for copy in copies:
        copy.wait()
    copy = pltpu.make_async_copy(held, out, sems.at[half])
    copy.start()
    copy.wait()


def receive_kernel(came, conv_one, proj_grad, gate_one_grad, made, sems):
    blocks = conv_one.shape[0]
    parts = math.gcd(blocks, PARTS)
    step = blocks // parts
    copies = [pltpu.make_async_copy(came.at[:, 1], proj_grad, sems.at[parts])]
    copies[0].start()
    for part in range(parts):
        here = pl.ds(part * step, step)
        made[here] = product(came[here, 0], conv_one[here])
        copies.append(pltpu.make_async_copy(made.at[here], gate_one_grad.at[here], sems.at[part]))
        copies[-1].start()
    for copy in copies:
        copy.wait()


def call(kernel, out_shape, scratch, flops, moved, *args, far=(), far_out=False, copies=0,
         limit=0):
    vmem = pl.BlockSpec(memory_space=pltpu.VMEM)
    smem = pl.BlockSpec(memory_space=pltpu.SMEM)
    hbm = pl.BlockSpec(memory_space=pltpu.HBM)
    held = sum(math.prod(dims) * np.dtype(dtype).itemsize for dims, dtype in scratch)
    buffers = [pltpu.VMEM(dims, dtype) for dims, dtype in scratch]
    if copies:
        buffers.append(pltpu.SemaphoreType.DMA((copies,)))
    return pl.pallas_call(
        kernel,
        out_shape=out_shape,
        in_specs=[smem if a.dtype == jnp.int32 else hbm if i in far else vmem
                  for i, a in enumerate(args)],
        out_specs=[hbm if far_out else vmem] * len(out_shape),
        scratch_shapes=buffers,
        compiler_params=pltpu.CompilerParams(
            vmem_limit_bytes=limit or held + SPARE),
        cost_estimate=pl.CostEstimate(flops=flops, bytes_accessed=moved, transcendentals=0),
    )(*args)


def exchange(value):
    return lax.all_to_all(value, "seq", split_axis=0, concat_axis=0, tiled=True)


def swap(value, step):
    count = lax.axis_size("seq")
    return lax.ppermute(value, "seq", [(j, j ^ step) for j in range(count)])


def local(
    out_grad,
    gate_one,
    gate_two,
    conv_one,
    conv_two,
    value,
    filter_one,
    filter_two,
    skip_one,
    skip_two,
    short_weight,
):
    blocks = lax.axis_size("seq")
    width = out_grad.shape[1]
    channels = filter_one.shape[0]
    length = filter_one.shape[1]
    rows = (blocks + 1) * channels
    shape = (blocks, channels, width)
    mat_hi, mat_lo, tw, tw_scaled = tables(
        blocks, width, length ** (-0.5) / (2 * length))
    work = 3 * 2 * rows * (2 * width) ** 2
    size = rows * 2 * width * 4

    def struct(*dims, dtype=F32):
        return jax.ShapeDtypeStruct(dims, dtype)

    groups = channels // ROWS
    tile = ((blocks + 1) * ROWS, 2 * width)
    halves = [((2,) + tile, BF16)] * 2
    back = ((2,) + tile, F32)
    spec = struct(groups, *tile)

    me = lax.axis_index("seq")
    taps = lax.dynamic_slice_in_dim(short_weight, me * channels, channels, axis=0)
    pair = struct(blocks, 2, channels, width, dtype=BF16)
    parts = math.gcd(blocks, PARTS)
    one = struct(*shape, dtype=BF16)
    triple = struct(blocks, 3, channels, width, dtype=BF16)
    first = exchange(call(
        send_kernel, [triple], [(shape, BF16)] * 5, 3 * pair.size, 7 * pair.size,
        *(a.reshape(shape) for a in (out_grad, gate_two, gate_one, value)),
        far=range(4), far_out=True, copies=7 * parts, limit=WHOLE)[0])
    half = blocks // 2
    half_shape = (half, channels, width)
    here = me[None].astype(jnp.int32)
    parts_of = call(
        pairs_kernel, [struct(2, channels, width, dtype=BF16)] * half,
        [(shape, BF16), (shape, BF16), ((half, 2, channels, width), BF16)],
        pair.size, 2 * pair.size, here, gate_one.reshape(shape), conv_one.reshape(shape),
        far=(1, 2), far_out=True, copies=half + 2, limit=WHOLE)
    came = [parts_of[0]] + [swap(parts_of[r], r) for r in range(1, half)]
    far = call(join_kernel, [struct(*half_shape, dtype=BF16)], [(half_shape, BF16)],
               pair.size, pair.size, *came, far=range(half), far_out=True, copies=half + 1,
               limit=WHOLE)[0]
    near = [part[:1] for part in came]
    h_one, h_two = call(
        functools.partial(spectrum_kernel, blocks, width),
        [spec, spec], halves, 2 * work, 4 * size,
        filter_one, filter_two, mat_hi, mat_lo, tw_scaled)
    gate_two_grad = product(out_grad, conv_two)
    far = swap(far, blocks // 2 + blocks // 4)
    first, h_one, h_two, gate_two_grad = lax.optimization_barrier(
        (first, h_one, h_two, gate_two_grad))
    grads, cg_one = call(
        functools.partial(adjoint_kernel, blocks, width),
        [pair, struct(*shape, dtype=BF16)],
        (halves + [back]) * 2 + [(pair.shape, BF16)] + [((groups,) + tile, F32)] * 2
        + [(pair.shape, BF16), (shape, BF16)],
        4 * work, 8 * size,
        first, h_two, h_one, skip_two[:, None], skip_one[:, None], taps, mat_hi, mat_lo, tw,
        far=(0, 1, 2), far_out=True, copies=6 * math.gcd(groups, PARTS), limit=WHOLE)
    cg_one, far = lax.optimization_barrier((cg_one, far))
    inner = jnp.concatenate(near + [far])
    third = exchange(grads)
    filter_one_grad, filter_two_grad = call(
        functools.partial(filter_kernel, blocks, width),
        [struct(channels, length), struct(channels, length)],
        halves * 2 + [back], 6 * work, 8 * size,
        here, first, inner, cg_one, mat_hi, mat_lo, tw, tw_scaled)
    proj_grad, gate_one_grad = call(
        receive_kernel, [one, one], [(shape, BF16)], pair.size, 6 * pair.size,
        third, conv_one.reshape(shape), far_out=True, copies=parts + 1)
    proj_grad = proj_grad.reshape(out_grad.shape)
    gate_one_grad = gate_one_grad.reshape(out_grad.shape)
    return (proj_grad, gate_one_grad, gate_two_grad, filter_one_grad, filter_two_grad)


def solution(mesh):
    frames = P(None, ("groups", "seq"))
    return jax.shard_map(
        local,
        mesh=mesh,
        in_specs=(frames,) * 6 + (P("seq", None),) * 2 + (P("seq"),) * 2 + (P(),),
        out_specs=(frames,) * 3 + (P(("groups", "seq"), None),) * 2,
        check_vma=False,
    )
```
